32 devices in a mesh: groups: 2 (over y), pool: 8 (over z, x), tensor: 2 (over core).
Axes of the slice: x: 2, y: 2, z: 4, core: 2. Of those that a mesh axis runs over, the one named last changes fastest.
Arguments:
- queries: bfloat16 [2, 16, 128, 4096], P(None, ('groups', 'pool'), None, 'tensor'), parts along dimension 1, may hold values from -140 to 140
- new_kv: bfloat16 [2, 16, 128, 1024], P(None, ('groups', 'pool'), None, 'tensor'), parts along dimension 1, may hold values from -6 to 6
- store: bfloat16 [2, 1024, 64, 1024], P(None, ('groups', 'pool'), None, 'tensor'), parts along dimension 1, may hold values from -6 to 6
- fetch_list: int32 [2, 16, 64, 2], P(None, 'groups'), parts along dimension 1, may hold values from 0 to 63, as said below
- prefix_blocks: int32 [16], P('groups'), parts along dimension 0, may hold values from 1 to 64, 204 in all
- writeback_map: int32 [2, 16, 2, 2], P(None, 'groups'), parts along dimension 1, may hold values from 0 to 7, as said below
Outputs:
- attention: bfloat16 [2, 16, 128, 4096], P(None, ('groups', 'pool'), None, 'tensor'), parts along dimension 1
- written: bfloat16 [2, 64, 64, 1024], P(None, ('groups', 'pool'), None, 'tensor'), parts along dimension 1
The draws below stay inside these ranges and needn't reach their ends.
There are 2 independent parts, one for each index of `groups`. The reference program is written for one: setup_inputs(seed, part) draws one part's arguments, and reference() takes and returns one part's arrays. A program takes and returns all parts, laid end to end along the dimension named above; each array names one. Nothing has to cross between parts.
Inputs may be any that keep to these rules, and one draw needn't show every extreme that they name: `fetch_list`: entry j of a session's list at a layer is used only where j is below the session's prefix_blocks. The used entries of one session name at most 8 blocks of one owner, and in every draw some session names exactly 8 of some owner. No two used entries of one layer name the same owner and slot. `writeback_map`: at each layer the 2 new blocks of session s go to distinct owners (s + (d mod 2) + (d div 2) * 2 * 2) mod 8 with 0 <= d < 4, each into slot d of that owner; in every layer some owner receives exactly 4 new blocks.
All inputs are finite; a program needn't handle non-finite values.
Results may differ from the reference program's by a relative error of at most 0.0071.
Values may be sent and summed in bfloat16 or wider, within the bound.
A program may use at most 192 MiB of HBM per device.

```python
import math
import jax
import jax.numpy as jnp
import numpy as np
from jax import lax

LAYERS = 2
HD = 128
KVH = 4
GROUP = 8
BLK = 64
NEW = 128
MAXB = 64
SESSIONS = 8
CAP = 8
NBNEW = 2
WSLOTS = 4


def raw_keys(key):
    return jnp.clip(jax.random.normal(jax.random.fold_in(key, 5), (LAYERS, SESSIONS, NEW, KVH, HD), jnp.float32), -4.5, 4.5)


def draw_new_kv(key, part):
    shared_keys = raw_keys(key)
    key = jax.random.fold_in(key, 31)
    values = jnp.clip(jax.random.normal(key, (LAYERS, SESSIONS, NEW, KVH, HD), jnp.float32), -6.0, 6.0)
    return jnp.stack([shared_keys, values], 4).reshape(LAYERS, SESSIONS, NEW, KVH * 2 * HD).astype(jnp.bfloat16)


def draw_queries(key, part):
    key = jax.random.fold_in(key, 37)
    base_key = jax.random.fold_in(key, 0)
    queried = 2.5 * jnp.clip(jax.random.normal(base_key, (LAYERS, SESSIONS, NEW, KVH, GROUP, HD), jnp.float32), -6.0, 6.0)
    return queried.reshape(LAYERS, SESSIONS, NEW, KVH * GROUP * HD).astype(jnp.bfloat16)


def permute_rows(keys_in, length):
    return jax.vmap(lambda subkey: jax.random.permutation(subkey, length))(keys_in)


def draw_fetch_list(key, part):
    key = jax.random.fold_in(key, 11)
    owner_key, spread_key, slot_key = jax.random.split(key, 3)
    total_rows = LAYERS * SESSIONS
    owner_perm = permute_rows(jax.random.split(owner_key, total_rows), SESSIONS).reshape(LAYERS, SESSIONS, SESSIONS)
    spread = permute_rows(jax.random.split(spread_key, total_rows), MAXB).reshape(LAYERS, SESSIONS, MAXB)
    slot_perm = permute_rows(jax.random.split(slot_key, total_rows), MAXB).reshape(LAYERS, SESSIONS, MAXB)
    owners = jnp.take_along_axis(owner_perm, spread % SESSIONS, axis=2)
    layer_ids = jnp.arange(LAYERS)[:, None, None]
    session_ids = jnp.arange(SESSIONS)[None, :, None]
    slot_ids = slot_perm[layer_ids, owners, session_ids * CAP + spread // SESSIONS]
    return jnp.stack([owners, slot_ids], -1).astype(jnp.int32)


def draw_writeback_map(key, part):
    key = jax.random.fold_in(key, 23)
    spacing = 2 * SESSIONS // WSLOTS
    lanes = jnp.arange(WSLOTS, dtype=jnp.int32)
    offset_table = lanes % 2 + lanes // 2 * spacing

    def one_layer(layer_key):
        offset_key, order_key, full_key = jax.random.split(layer_key, 3)
        offset_perm = permute_rows(jax.random.split(offset_key, SESSIONS), WSLOTS)
        block_order = permute_rows(jax.random.split(order_key, SESSIONS), NBNEW)
        full_owner = jax.random.randint(full_key, (), 0, SESSIONS)
        session_ids = jnp.arange(SESSIONS, dtype=jnp.int32)
        apart = (full_owner - session_ids) % SESSIONS
        matches = offset_table[None, :] == apart[:, None]
        is_forced = jnp.any(matches, 1)
        forced = jnp.argmax(matches, axis=1)
        spot = jnp.argmax(offset_perm == forced[:, None], axis=1)
        rolled = jnp.take_along_axis(offset_perm, (spot[:, None] + lanes[None, :]) % WSLOTS, axis=1)
        chosen = jnp.where(is_forced[:, None], rolled, offset_perm)[:, :NBNEW]
        slots = jnp.take_along_axis(chosen, block_order, axis=1)
        owners = (session_ids[:, None] + offset_table[slots]) % SESSIONS
        return jnp.stack([owners, slots], -1)
    return jax.vmap(one_layer)(jax.random.split(key, LAYERS)).astype(jnp.int32)


def block_scale(key, extent, pieces, low, top_value):
    def one(axis_at, parts):
        draws = jax.random.uniform(jax.random.fold_in(jax.random.fold_in(key, 6), axis_at), (parts,), jnp.float32, low / len(pieces), top_value / len(pieces))
        return jnp.repeat(jnp.exp(draws), extent[axis_at] // parts).reshape((-1,) + (1,) * (len(extent) - axis_at - 1))

    factor_of = one(*pieces[0])
    for cut in pieces[1:]:
        factor_of = factor_of * one(*cut)
    return factor_of


def profile(number_of, total, limit, lean):
    weights = [(1 << 20) // math.isqrt(standing ** lean) + 1 for standing in range(2, number_of + 1)]
    rest, given = total - limit - (number_of - 1), [1] * (number_of - 1)
    while rest > 0:
        candidates = [i for i in range(number_of - 1) if given[i] < limit]
        mass, budget = sum([weights[i] for i in candidates]), rest
        for i in candidates:
            extra = min(limit - given[i], max(1, budget * weights[i] // mass), rest)
            given[i] = given[i] + extra
            rest = rest - extra
    return np.array([limit] + given)


def uneven_parts(rng, amount, total, bound, slope):
    if amount == 2:
        one = jax.random.randint(rng, (), max(1, total - bound), min(bound, total - 1) + 1)
        return jnp.stack([one, total - one])
    tallies = jnp.asarray(profile(amount, total, bound, slope), jnp.int32)
    couples = (amount - 1) // 2
    donor, taker = tallies[1:1 + 2 * couples:2], tallies[2:2 + 2 * couples:2]
    margin = jnp.minimum(donor - 1, bound - taker)
    moved = jax.random.randint(jax.random.fold_in(rng, 1), (couples,), 0, 1 << 20) % (margin + 1)
    tallies = tallies.at[1:1 + 2 * couples:2].set(donor - moved).at[2:2 + 2 * couples:2].set(taker + moved)
    return tallies[jax.random.permutation(jax.random.fold_in(rng, 2), amount)]


def scatter_about(own_key, dims, width, most, cuts=(), kind=jnp.bfloat16):
    values = jax.random.normal(own_key, dims, jnp.float32) * width
    if len(cuts) > 0:
        values = block_scale(own_key, dims, cuts, -0.22, 0.18) * values
    return jnp.clip(values, min=-most, max=most).astype(kind)


def setup_inputs(seed: int = 0, part: int = 0) -> dict:
    keys = jax.random.split(jax.random.key(seed), 7)
    own_keys = jax.random.split(jax.random.fold_in(keys[6], part), 7)
    queries = draw_queries(jax.random.fold_in(jax.random.fold_in(keys[6], part), 71), part)
    new_kv = draw_new_kv(jax.random.fold_in(jax.random.fold_in(keys[6], part), 71), part)
    store = scatter_about(own_keys[2], (LAYERS, SESSIONS * MAXB, BLK, KVH * 2 * HD), 1.0, 6.0, ((1, 8), (3, 2)))
    fetch_list = draw_fetch_list(jax.random.fold_in(jax.random.fold_in(keys[6], part), 71), part)
    prefix_blocks = uneven_parts(own_keys[4], SESSIONS, SESSIONS * MAXB * 2 // 5, MAXB, 2).astype(jnp.int32)
    writeback_map = draw_writeback_map(jax.random.fold_in(jax.random.fold_in(keys[6], part), 71), part)
    return {"queries": queries, "new_kv": new_kv, "store": store, "fetch_list": fetch_list, "prefix_blocks": prefix_blocks, "writeback_map": writeback_map}


def rotate(source, places):
    half_width = source.shape[-1] // 2
    frequencies = 500000.0 ** (-(jnp.arange(half_width, dtype=jnp.float32) * 2.0 / source.shape[-1]))
    angles = places[..., None] * frequencies
    cosine = jnp.cos(angles)
    sine_part = jnp.sin(angles)
    first_half = source[..., :half_width]
    second = source[..., half_width:]
    return jnp.concatenate([first_half * cosine - second * sine_part, second * cosine + first_half * sine_part], -1)


def reference(queries, new_kv, store, fetch_list, prefix_blocks, writeback_map):
    score_scale = HD ** -0.5
    attention_all = []
    written_all = []
    for layer_index in range(LAYERS):
        def session(session_id):
            length = prefix_blocks[session_id]
            places = (length * BLK + jnp.arange(NEW, dtype=jnp.int32)).astype(jnp.float32)
            rotated_query = rotate(queries[layer_index, session_id].reshape(NEW, KVH, GROUP, HD).astype(jnp.float32), places[:, None, None]).astype(jnp.bfloat16)
            fresh_rows = new_kv[layer_index, session_id].reshape(NEW, KVH, 2, HD)
            new_keys = rotate(fresh_rows[:, :, 0].astype(jnp.float32), places[:, None]).astype(jnp.bfloat16)
            values = fresh_rows[:, :, 1]
            fetch_rows = (fetch_list[layer_index, session_id, :, 0] * MAXB + fetch_list[layer_index, session_id, :, 1]).astype(jnp.int32)
            prefix = jnp.take(store[layer_index], fetch_rows, axis=0).reshape(MAXB * BLK, KVH, 2, HD)
            all_keys = jnp.concatenate([prefix[:, :, 0], new_keys], 0).astype(jnp.float32)
            all_values = jnp.concatenate([prefix[:, :, 1], values], 0).astype(jnp.float32)
            kept_keys = jnp.repeat(jnp.arange(MAXB, dtype=jnp.int32) < length, BLK)
            token_ids = jnp.arange(NEW, dtype=jnp.int32)
            causal = token_ids[None, :] <= token_ids[:, None]
            allowed = jnp.concatenate([jnp.broadcast_to(kept_keys[None, :], (NEW, MAXB * BLK)), causal], 1)
            scores = jnp.einsum("tkgd,nkd->kgtn", rotated_query.astype(jnp.float32), all_keys) * score_scale
            scores = jnp.where(allowed[None, None], scores, -jnp.inf)
            row_top = jnp.max(scores, -1, keepdims=True)
            weights = jnp.exp(scores - row_top)
            row_total = jnp.sum(weights, -1)
            rounded = lax.optimization_barrier(weights.astype(jnp.bfloat16)).astype(jnp.float32)
            mixture = jnp.einsum("kgtn,nkd->tkgd", rounded, all_values)
            mixture = mixture / jnp.transpose(row_total, (2, 0, 1))[..., None]
            attention = mixture.astype(jnp.bfloat16).reshape(NEW, KVH * GROUP * HD)
            blocks = jnp.stack([new_keys, values], 2).reshape(NBNEW, BLK, KVH * 2 * HD)
            return attention, blocks

        attention, blocks = lax.map(session, jnp.arange(SESSIONS, dtype=jnp.int32))
        target_rows = (writeback_map[layer_index, :, :, 0] * WSLOTS + writeback_map[layer_index, :, :, 1]).reshape(-1).astype(jnp.int32)
        written = jnp.zeros((SESSIONS * WSLOTS, BLK, KVH * 2 * HD), jnp.bfloat16)
        written = written.at[target_rows].set(blocks.reshape(SESSIONS * NBNEW, BLK, KVH * 2 * HD))
        attention_all.append(attention)
        written_all.append(written)
    return jnp.stack(attention_all), jnp.stack(written_all)
```

```python
import functools

import jax
import jax.numpy as jnp
from jax import lax
from jax.experimental import pallas as pl
from jax.experimental.pallas import tpu as pltpu
from jax.sharding import PartitionSpec as P

HD = 128
GROUP = 8
MAXB = 64
NBNEW = 2
WSLOTS = 4


def rotate(source, places):
    half_width = source.shape[-1] // 2
    frequencies = 500000.0 ** (
        -(jnp.arange(half_width, dtype=jnp.float32) * 2.0 / source.shape[-1])
    )
    angles = places[..., None] * frequencies
    cosine = jnp.cos(angles)
    sine_part = jnp.sin(angles)
    first_half = source[..., :half_width]
    second = source[..., half_width:]
    return jnp.concatenate(
        [first_half * cosine - second * sine_part, second * cosine + first_half * sine_part], -1
    )


def per_device(queries, new_kv, store, fetch_list, prefix_blocks, writeback_map):
    pool_size = lax.axis_size("pool")
    my_index = lax.axis_index("pool")
    layer_count = queries.shape[0]
    new_count = queries.shape[2]
    block_len = store.shape[2]
    row_width = store.shape[3]
    kv_local = row_width // (2 * HD)
    per_owner = MAXB // pool_size
    score_scale = HD ** (-0.5)
    length = prefix_blocks[my_index]
    places = (length * block_len + jnp.arange(new_count, dtype=jnp.int32)).astype(jnp.float32)
    block_order = jnp.arange(MAXB, dtype=jnp.int32)
    earlier = block_order[None, :] < block_order[:, None]
    live_entries = block_order[None, :] < prefix_blocks[:, None]
    lane_ids = jnp.arange(per_owner, dtype=jnp.int32)
    sources = jnp.arange(pool_size, dtype=jnp.int32)
    slot_range = jnp.arange(WSLOTS, dtype=jnp.int32)
    token_ids = jnp.arange(new_count, dtype=jnp.int32)
    causal_rows = jnp.repeat(token_ids[None, :] <= token_ids[:, None], GROUP, axis=0)
    attention_all = []
    written_all = []
    for layer_index in range(layer_count):
        owners = fetch_list[layer_index, :, :, 0]
        slot_ids = fetch_list[layer_index, :, :, 1]
        owner_rank = jnp.sum((owners[:, :, None] == owners[:, None, :]) & earlier[None], -1)
        chosen = ((owners == my_index) & live_entries)[:, None, :] & (
            owner_rank[:, None, :] == lane_ids[None, :, None]
        )
        picked = jnp.sum(jnp.where(chosen, slot_ids[:, None, :], 0), -1).reshape(-1)
        present = jnp.any(chosen, -1).reshape(-1)
        picked_rows = jnp.take(store[layer_index], picked, axis=0)
        outgoing = jnp.where(present[:, None, None], picked_rows, jnp.zeros_like(picked_rows))
        arrival = (
            (owners[my_index][:, None, None] == sources[None, :, None])
            & (owner_rank[my_index][:, None, None] == lane_ids[None, None, :])
            & live_entries[my_index][:, None, None]
        )
        outgoing, prefix_ok = (outgoing, jnp.any(arrival, 0).reshape(-1))
        prefix = lax.all_to_all(outgoing, "pool", split_axis=0, concat_axis=0, tiled=True)
        rotated_query = rotate(
            queries[layer_index, 0].reshape(new_count, kv_local, GROUP, HD).astype(jnp.float32),
            places[:, None, None],
        ).astype(jnp.bfloat16)
        fresh_rows = new_kv[layer_index, 0].reshape(new_count, kv_local, 2, HD)
        new_keys = rotate(fresh_rows[:, :, 0].astype(jnp.float32), places[:, None]).astype(
            jnp.bfloat16
        )
        values = fresh_rows[:, :, 1]
        key_count = prefix.shape[0] * prefix.shape[1]
        flat_prefix = prefix.reshape(key_count, kv_local, 2, HD)
        kept_keys = jnp.repeat(prefix_ok, prefix.shape[1])
        results = []
        for head_index in range(kv_local):
            query_rows = rotated_query[:, head_index].reshape(new_count * GROUP, HD)
            far_scores = (
                jnp.einsum(
                    "rd,nd->rn",
                    query_rows,
                    flat_prefix[:, head_index, 0],
                    preferred_element_type=jnp.float32,
                )
                * score_scale
            )
            near_scores = (
                jnp.einsum(
                    "rd,nd->rn",
                    query_rows,
                    new_keys[:, head_index],
                    preferred_element_type=jnp.float32,
                )
                * score_scale
            )
            far_scores = jnp.where(kept_keys[None, :], far_scores, -jnp.inf)
            near_scores = jnp.where(causal_rows, near_scores, -jnp.inf)
            row_top = jnp.maximum(jnp.max(far_scores, -1), jnp.max(near_scores, -1))
            far_weights = jnp.exp(far_scores - row_top[:, None])
            near_weights = jnp.exp(near_scores - row_top[:, None])
            row_total = jnp.sum(far_weights, -1) + jnp.sum(near_weights, -1)
            mixture = jnp.einsum(
                "rn,nd->rd",
                far_weights.astype(jnp.bfloat16),
                flat_prefix[:, head_index, 1],
                preferred_element_type=jnp.float32,
            )
            mixture = mixture + jnp.einsum(
                "rn,nd->rd",
                near_weights.astype(jnp.bfloat16),
                values[:, head_index],
                preferred_element_type=jnp.float32,
            )
            results.append((mixture / row_total[:, None]).reshape(new_count, GROUP, HD))
        attention = (
            jnp.stack(results, 1).reshape(new_count, kv_local * GROUP * HD).astype(jnp.bfloat16)
        )
        attend_blocks = jnp.stack([new_keys, values], 2).reshape(NBNEW, block_len * row_width)
        attention, blocks = (attention, attend_blocks)
        attention_all.append(attention)
        targets = writeback_map[layer_index, :, :, 0]
        target_slots = writeback_map[layer_index, :, :, 1]
        flat_targets = targets.reshape(-1)
        flat_slots = target_slots.reshape(-1)
        selector = (
            (flat_targets == my_index)[None, :] & (flat_slots[None, :] == slot_range[:, None])
        ).astype(jnp.bfloat16)
        stored = jnp.dot(
            selector,
            lax.all_gather(blocks, "pool", axis=0, tiled=True),
            preferred_element_type=jnp.float32,
        )
        written_all.append(stored.astype(jnp.bfloat16).reshape(WSLOTS, block_len, row_width))
    return (jnp.stack(attention_all)[:, None], jnp.stack(written_all))

EMPTY = -1e30
EXP_SCALE = HD ** (-0.5) * 1.4426950408889634
GATHERED = 4


def partial_kernel(block_len, near, counts, q_ref, *refs):
    if near:
        new_ref, local_ref, other_ref, out_ref, stat_ref, top, total, acc = refs
    else:
        local_ref, other_ref, out_ref, stat_ref, top, total, acc = refs
    rows = q_ref.shape[1]

    def add(kv, keep):
        q = q_ref[0]
        s = lax.dot_general(
            kv[:, :HD], q, (((1,), (1,)), ((), ())), preferred_element_type=jnp.float32
        )
        s = jnp.where(keep(s.shape), s, EMPTY)
        old = top[...]
        fresh = jnp.maximum(old, jnp.max(s, 0, keepdims=True))
        p = jnp.exp2((s - fresh) * EXP_SCALE)
        fade = jnp.exp2((old - fresh) * EXP_SCALE)
        total[...] = total[...] * fade + jnp.sum(p, 0, keepdims=True)
        acc[...] = acc[...] * fade + lax.dot_general(
            kv[:, HD:],
            p.astype(jnp.bfloat16),
            (((0,), (0,)), ((), ())),
            preferred_element_type=jnp.float32,
        )
        top[...] = fresh

    top[...] = jnp.full((1, rows), EMPTY, jnp.float32)
    total[...] = jnp.zeros((1, rows), jnp.float32)
    acc[...] = jnp.zeros((HD, rows), jnp.float32)
    if near:
        new_count = new_ref.shape[0]

        def causal(shape):
            token = lax.broadcasted_iota(jnp.int32, shape, 1) % new_count
            return lax.broadcasted_iota(jnp.int32, shape, 0) <= token

        add(new_ref[...], causal)
    for which, ref in ((1, local_ref), (2, other_ref)):
        held = ref.shape[1] // block_len
        for first in range(0, held, GATHERED):
            last = min(held, first + GATHERED)
            left = counts[which] - first

            @pl.when(left > 0)
            def _(ref=ref, first=first, last=last, left=left):
                add(
                    ref[0, first * block_len : last * block_len, :],
                    lambda shape: lax.broadcasted_iota(jnp.int32, shape, 0) < left * block_len,
                )

    out_ref[0] = acc[...].astype(jnp.bfloat16)
    stat_ref[0, 0:1] = top[...]
    stat_ref[0, 1:2] = total[...]


def partial_attention(row, local_count, other_count, q, local, other, block_len, new=None):
    heads, rows, _ = q.shape
    kept = local.shape[1]
    counts = jnp.stack([row, local_count, other_count]).astype(jnp.int32)
    kv_spec = pl.BlockSpec((1, kept, 2 * HD), lambda h, c: (c[0], 0, h))
    specs = [pl.BlockSpec((1, rows, HD), lambda h, c: (h, 0, 0))]
    arrays = [q]
    if new is not None:
        specs.append(pl.BlockSpec((new.shape[0], 2 * HD), lambda h, c: (0, h)))
        arrays.append(new)
    return pl.pallas_call(
        functools.partial(partial_kernel, block_len, new is not None),
        out_shape=(
            jax.ShapeDtypeStruct((heads, HD, rows), jnp.bfloat16),
            jax.ShapeDtypeStruct((heads, 2, rows), jnp.float32),
        ),
        grid_spec=pltpu.PrefetchScalarGridSpec(
            num_scalar_prefetch=1,
            grid=(heads,),
            in_specs=specs + [kv_spec, kv_spec],
            out_specs=(
                pl.BlockSpec((1, HD, rows), lambda h, c: (h, 0, 0)),
                pl.BlockSpec((1, 2, rows), lambda h, c: (h, 0, 0)),
            ),
            scratch_shapes=[
                pltpu.VMEM((1, rows), jnp.float32),
                pltpu.VMEM((1, rows), jnp.float32),
                pltpu.VMEM((HD, rows), jnp.float32),
            ],
        ),
        compiler_params=pltpu.CompilerParams(vmem_limit_bytes=32 * 1024 * 1024),
        cost_estimate=pl.CostEstimate(
            flops=heads * rows * kept * HD * 4,
            bytes_accessed=heads * (rows * HD + kept * HD * 2) * 4,
            transcendentals=heads * rows * kept,
        ),
    )(counts, *arrays, local, other)


def merge(parts):
    tops = [jnp.where(stat[:, 1:2] > 0, stat[:, 0:1], EMPTY) for _, stat in parts]
    top = functools.reduce(jnp.maximum, tops)
    scales = [jnp.exp2((one - top) * EXP_SCALE) for one in tops]
    out = sum(part[0].astype(jnp.float32) * scale for part, scale in zip(parts, scales))
    total = sum(part[1][:, 1:2] * scale for part, scale in zip(parts, scales))
    return out, top, total


def packed(parts):
    out, top, total = merge(parts)
    return out.astype(jnp.bfloat16), jnp.concatenate([top, total], 1)


def per_device_rows(pool_size, queries, new_kv, store, fetch_list, prefix_blocks, writeback_map):
    pair_count = pool_size // 2
    me = lax.axis_index("pool")
    line, side = me // 2, me % 2
    layers, _, new_count, _ = queries.shape
    sessions = prefix_blocks.shape[0]
    slots, block_len, row_width = store.shape[1:]
    heads = row_width // (2 * HD)
    cap = MAXB // pool_size

    def send(array, pairs):
        moves = [(2 * a + s, 2 * b + s) for a, b in pairs for s in range(2)]
        return jax.tree.map(lambda one: lax.ppermute(one, "pool", moves), array)

    length = prefix_blocks[me]
    places = (length * block_len + jnp.arange(new_count, dtype=jnp.int32)).astype(jnp.float32)
    asked = []
    for layer in range(layers):
        turned = rotate(
            queries[layer, 0].reshape(new_count, heads, GROUP, HD).astype(jnp.float32),
            places[:, None, None],
        ).astype(jnp.bfloat16)
        asked.append(turned.transpose(1, 2, 0, 3).reshape(heads, GROUP * new_count, HD))

    live = jnp.arange(MAXB, dtype=jnp.int32)[None, :] < prefix_blocks[:, None]
    earlier = jnp.triu(jnp.ones((MAXB, MAXB), jnp.float32), 1)

    def used(owner):
        return (fetch_list[..., 0] == owner) & live[None]

    mine = used(me)
    rank = jnp.dot(mine.astype(jnp.float32), earlier).astype(jnp.int32)
    lanes = jnp.arange(cap, dtype=jnp.int32)
    chosen = mine[:, :, None, :] & (rank[:, :, None, :] == lanes[:, None])
    picked = jnp.sum(jnp.where(chosen, fetch_list[:, :, None, :, 1], 0), -1)
    picked = picked + (jnp.arange(layers, dtype=jnp.int32) * slots)[:, None, None]
    picked = picked.reshape(layers, pair_count, 2, cap)
    by_side = lambda a: jnp.sum(a.astype(jnp.int32), -1).reshape(layers, pair_count, 2)
    local_counts = lax.dynamic_index_in_dim(by_side(mine), side, 2, False)
    other_counts = lax.dynamic_index_in_dim(by_side(used(me + 1 - 2 * side)), side, 2, False)
    own_picks = lax.dynamic_index_in_dim(picked, side, 2, False)
    sent_picks = lax.dynamic_index_in_dim(picked, 1 - side, 2, False)
    flat_store = store.reshape(layers * slots, block_len, row_width)

    def blocks_of(picks):
        return jnp.take(flat_store, picks.reshape(-1), axis=0, mode="clip").reshape(
            pair_count, cap * block_len, row_width
        )

    swap = [(i, i + 1 - 2 * (i % 2)) for i in range(pool_size)]
    fresh = new_kv[:, 0].reshape(layers, new_count, heads, 2, HD)
    new_keys = rotate(fresh[:, :, :, 0].astype(jnp.float32), places[:, None]).astype(jnp.bfloat16)
    new_rows = jnp.stack([new_keys, fresh[:, :, :, 1]], 3).reshape(layers, new_count, row_width)

    other, local, rows_of = [], [], []
    for layer in range(layers):
        other.append(lax.ppermute(blocks_of(sent_picks[layer]), "pool", swap))
        local.append(blocks_of(own_picks[layer]))
        down = up = asked[layer]
        from_up, from_down = {}, {}
        for step in range(1, pair_count):
            down = send(down, [(a, a - 1) for a in range(1, pair_count) if a + step <= pair_count])
            up = send(up, [(a, a + 1) for a in range(pair_count - 1) if a - step + 1 >= 0])
            from_up[step], from_down[step] = down, up
        rows_of.append(
            [asked[layer]]
            + [
                jnp.where(line + t < pair_count, from_up[t], from_down[pair_count - t])
                for t in range(1, pair_count)
            ]
        )

    attention_all = []
    for layer in range(layers):
        parts = {}
        for t in sorted(range(pair_count), key=lambda t: -min(t, pair_count - t) if t else 1):
            row = (line + t) % pair_count
            parts[t] = partial_attention(
                row,
                local_counts[layer][row],
                other_counts[layer][row],
                rows_of[layer][t],
                local[layer],
                other[layer],
                block_len,
                new_rows[layer] if t == 0 else None,
            )
        down = up = None
        for step in range(1, pair_count):
            lower = [parts[step]] + ([down] if down else [])
            upper = [parts[pair_count - step]] + ([up] if up else [])
            lower = packed(lower) if down else parts[step]
            upper = packed(upper) if up else parts[pair_count - step]
            down = send(lower, [(a, a - 1) for a in range(1, pair_count) if a + step >= pair_count])
            up = send(upper, [(a, a + 1) for a in range(pair_count - 1) if a < step])
        out, _, total = merge([parts[0], down, up])
        out = (out / total).astype(jnp.bfloat16).reshape(heads, HD, GROUP, new_count)
        attention_all.append(out.transpose(3, 0, 2, 1).reshape(new_count, heads * GROUP * HD))

    new_blocks = new_rows.reshape(layers, NBNEW, block_len, row_width)
    slot_of = writeback_map[:, me, :, 1]
    written = []
    for d in range(WSLOTS):
        block = jnp.zeros((layers, block_len, row_width), jnp.bfloat16)
        for b in range(NBNEW):
            block = jnp.where((slot_of[:, b] == d)[:, None, None], new_blocks[:, b], block)
        shift = d % 2 + d // 2 * (2 * pool_size // WSLOTS)
        if shift % pool_size:
            block = lax.ppermute(
                block, "pool", [(i, (i + shift) % pool_size) for i in range(pool_size)]
            )
        written.append(block)
    return jnp.stack(attention_all)[:, None], jnp.stack(written, 1)


def solution(mesh):
    pool_size = mesh.shape["pool"]
    if pool_size % 2 == 0 and MAXB // pool_size >= 4:
        plan = functools.partial(per_device_rows, pool_size)
    else:
        plan = per_device
    in_specs = (
        P(None, ("groups", "pool"), None, "tensor"),
        P(None, ("groups", "pool"), None, "tensor"),
        P(None, ("groups", "pool"), None, "tensor"),
        P(None, "groups", None, None),
        P("groups"),
        P(None, "groups", None, None),
    )
    out_specs = (
        P(None, ("groups", "pool"), None, "tensor"),
        P(None, ("groups", "pool"), None, "tensor"),
    )
    return jax.shard_map(
        plan, mesh=mesh, in_specs=in_specs, out_specs=out_specs, check_vma=False
    )
```

```python
import functools

import jax
import jax.numpy as jnp
from jax import lax
from jax.experimental import pallas as pl
from jax.experimental.pallas import tpu as pltpu
from jax.sharding import PartitionSpec as P

HD = 128
GROUP = 8
MAXB = 64
NBNEW = 2
WSLOTS = 4


def rotate(source, places):
    half_width = source.shape[-1] // 2
    frequencies = 500000.0 ** (
        -(jnp.arange(half_width, dtype=jnp.float32) * 2.0 / source.shape[-1])
    )
    angles = places[..., None] * frequencies
    cosine = jnp.cos(angles)
    sine_part = jnp.sin(angles)
    first_half = source[..., :half_width]
    second = source[..., half_width:]
    return jnp.concatenate(
        [first_half * cosine - second * sine_part, second * cosine + first_half * sine_part], -1
    )


def per_device(queries, new_kv, store, fetch_list, prefix_blocks, writeback_map):
    pool_size = lax.axis_size("pool")
    my_index = lax.axis_index("pool")
    layer_count = queries.shape[0]
    new_count = queries.shape[2]
    block_len = store.shape[2]
    row_width = store.shape[3]
    kv_local = row_width // (2 * HD)
    per_owner = MAXB // pool_size
    score_scale = HD ** (-0.5)
    length = prefix_blocks[my_index]
    places = (length * block_len + jnp.arange(new_count, dtype=jnp.int32)).astype(jnp.float32)
    block_order = jnp.arange(MAXB, dtype=jnp.int32)
    earlier = block_order[None, :] < block_order[:, None]
    live_entries = block_order[None, :] < prefix_blocks[:, None]
    lane_ids = jnp.arange(per_owner, dtype=jnp.int32)
    sources = jnp.arange(pool_size, dtype=jnp.int32)
    slot_range = jnp.arange(WSLOTS, dtype=jnp.int32)
    token_ids = jnp.arange(new_count, dtype=jnp.int32)
    causal_rows = jnp.repeat(token_ids[None, :] <= token_ids[:, None], GROUP, axis=0)
    attention_all = []
    written_all = []
    for layer_index in range(layer_count):
        owners = fetch_list[layer_index, :, :, 0]
        slot_ids = fetch_list[layer_index, :, :, 1]
        owner_rank = jnp.sum((owners[:, :, None] == owners[:, None, :]) & earlier[None], -1)
        chosen = ((owners == my_index) & live_entries)[:, None, :] & (
            owner_rank[:, None, :] == lane_ids[None, :, None]
        )
        picked = jnp.sum(jnp.where(chosen, slot_ids[:, None, :], 0), -1).reshape(-1)
        present = jnp.any(chosen, -1).reshape(-1)
        picked_rows = jnp.take(store[layer_index], picked, axis=0)
        outgoing = jnp.where(present[:, None, None], picked_rows, jnp.zeros_like(picked_rows))
        arrival = (
            (owners[my_index][:, None, None] == sources[None, :, None])
            & (owner_rank[my_index][:, None, None] == lane_ids[None, None, :])
            & live_entries[my_index][:, None, None]
        )
        outgoing, prefix_ok = (outgoing, jnp.any(arrival, 0).reshape(-1))
        prefix = lax.all_to_all(outgoing, "pool", split_axis=0, concat_axis=0, tiled=True)
        rotated_query = rotate(
            queries[layer_index, 0].reshape(new_count, kv_local, GROUP, HD).astype(jnp.float32),
            places[:, None, None],
        ).astype(jnp.bfloat16)
        fresh_rows = new_kv[layer_index, 0].reshape(new_count, kv_local, 2, HD)
        new_keys = rotate(fresh_rows[:, :, 0].astype(jnp.float32), places[:, None]).astype(
            jnp.bfloat16
        )
        values = fresh_rows[:, :, 1]
        key_count = prefix.shape[0] * prefix.shape[1]
        flat_prefix = prefix.reshape(key_count, kv_local, 2, HD)
        kept_keys = jnp.repeat(prefix_ok, prefix.shape[1])
        results = []
        for head_index in range(kv_local):
            query_rows = rotated_query[:, head_index].reshape(new_count * GROUP, HD)
            far_scores = (
                jnp.einsum(
                    "rd,nd->rn",
                    query_rows,
                    flat_prefix[:, head_index, 0],
                    preferred_element_type=jnp.float32,
                )
                * score_scale
            )
            near_scores = (
                jnp.einsum(
                    "rd,nd->rn",
                    query_rows,
                    new_keys[:, head_index],
                    preferred_element_type=jnp.float32,
                )
                * score_scale
            )
            far_scores = jnp.where(kept_keys[None, :], far_scores, -jnp.inf)
            near_scores = jnp.where(causal_rows, near_scores, -jnp.inf)
            row_top = jnp.maximum(jnp.max(far_scores, -1), jnp.max(near_scores, -1))
            far_weights = jnp.exp(far_scores - row_top[:, None])
            near_weights = jnp.exp(near_scores - row_top[:, None])
            row_total = jnp.sum(far_weights, -1) + jnp.sum(near_weights, -1)
            mixture = jnp.einsum(
                "rn,nd->rd",
                far_weights.astype(jnp.bfloat16),
                flat_prefix[:, head_index, 1],
                preferred_element_type=jnp.float32,
            )
            mixture = mixture + jnp.einsum(
                "rn,nd->rd",
                near_weights.astype(jnp.bfloat16),
                values[:, head_index],
                preferred_element_type=jnp.float32,
            )
            results.append((mixture / row_total[:, None]).reshape(new_count, GROUP, HD))
        attention = (
            jnp.stack(results, 1).reshape(new_count, kv_local * GROUP * HD).astype(jnp.bfloat16)
        )
        attend_blocks = jnp.stack([new_keys, values], 2).reshape(NBNEW, block_len * row_width)
        attention, blocks = (attention, attend_blocks)
        attention_all.append(attention)
        targets = writeback_map[layer_index, :, :, 0]
        target_slots = writeback_map[layer_index, :, :, 1]
        flat_targets = targets.reshape(-1)
        flat_slots = target_slots.reshape(-1)
        selector = (
            (flat_targets == my_index)[None, :] & (flat_slots[None, :] == slot_range[:, None])
        ).astype(jnp.bfloat16)
        stored = jnp.dot(
            selector,
            lax.all_gather(blocks, "pool", axis=0, tiled=True),
            preferred_element_type=jnp.float32,
        )
        written_all.append(stored.astype(jnp.bfloat16).reshape(WSLOTS, block_len, row_width))
    return (jnp.stack(attention_all)[:, None], jnp.stack(written_all))

EMPTY = -1e30
EXP_SCALE = HD ** (-0.5) * 1.4426950408889634
MASKED = -2e30


def gather_kernel(picks, store_ref, out_ref, sems):
    count = out_ref.shape[0]

    def copy(i):
        return pltpu.make_async_copy(store_ref.at[picks[i]], out_ref.at[i], sems.at[i])

    lax.fori_loop(0, count, lambda i, x: (copy(i).start(), x)[1], 0)
    lax.fori_loop(0, count, lambda i, x: (copy(i).wait(), x)[1], 0)


def gather_blocks(picks, flat_store):
    return pl.pallas_call(
        gather_kernel,
        out_shape=jax.ShapeDtypeStruct(picks.shape + flat_store.shape[1:], flat_store.dtype),
        grid_spec=pltpu.PrefetchScalarGridSpec(
            num_scalar_prefetch=1,
            grid=(),
            in_specs=[pl.BlockSpec(memory_space=pl.ANY)],
            out_specs=pl.BlockSpec(memory_space=pl.ANY),
            scratch_shapes=[pltpu.SemaphoreType.DMA(picks.shape)],
        ),
    )(picks, flat_store)


def shift_of(d, pool_size):
    return d % 2 + d // 2 * (2 * pool_size // WSLOTS)


def pair_kernel(
    pool_size, block_len, counts, q_ref, sent_ref, local_ref, new_ref, back_ref,
    out_ref, written_ref,
    q_all, other, part, stat, low, low_stat, high, high_stat, landed,
    kv_send, kv_recv, q_send, q_recv, p_send, p_recv, w_send, w_recv,
):
    pairs = pool_size // 2
    layers, heads, rows, _ = q_ref.shape
    new_count = new_ref.shape[1]
    kept = local_ref.shape[2]
    me = lax.axis_index("pool")
    line = me // 2
    partner = me + 1 - 2 * (me % 2)

    def remote(src, dst, send, recv, device):
        return pltpu.make_async_remote_copy(
            src_ref=src, dst_ref=dst, send_sem=send, recv_sem=recv,
            device_id={"pool": device}, device_id_type=pl.DeviceIdType.MESH,
        )

    barrier = pltpu.get_barrier_semaphore()
    for k in range(1, pool_size):
        pl.semaphore_signal(
            barrier, inc=1, device_id={"pool": lax.rem(me + k, pool_size)},
            device_id_type=pl.DeviceIdType.MESH,
        )
    pl.semaphore_wait(barrier, pool_size - 1)

    def kv_copy(l, t):
        return remote(
            sent_ref.at[l, t], other.at[l, t], kv_send.at[l, t], kv_recv.at[l, t], partner
        )

    def q_down(l, step):
        src = q_ref.at[l] if step == 1 else q_all.at[l, step - 1]
        return remote(
            src, q_all.at[l, step], q_send.at[l, 0, step], q_recv.at[l, step],
            lax.rem(me + pool_size - 2, pool_size),
        )

    def q_up(l, step):
        src = q_ref.at[l] if step == 1 else q_all.at[l, pairs - step + 1]
        return remote(
            src, q_all.at[l, pairs - step], q_send.at[l, 1, step], q_recv.at[l, pairs - step],
            lax.rem(me + 2, pool_size),
        )

    def goes_down(step):
        return (line >= 1) & (line + step <= pairs)

    def goes_up(step):
        return (line <= pairs - 2) & (line - step + 1 >= 0)

    def back_copy(d):
        device = lax.rem(me + shift_of(d, pool_size), pool_size)
        return remote(back_ref.at[d], landed.at[d], w_send.at[d], w_recv.at[d], device)

    def q_step(l, step):
        @pl.when(goes_down(step))
        def _():
            if step > 1:
                q_down(l, step - 1).wait_recv()
            q_down(l, step).start()

        @pl.when(goes_up(step))
        def _():
            if step > 1:
                q_up(l, step - 1).wait_recv()
            q_up(l, step).start()

    def wait_query(l, t):
        from_above = line + t <= pairs - 1
        passed = jnp.where(from_above, goes_down(t + 1), goes_up(pairs - t + 1))

        @pl.when(jnp.logical_not(passed))
        def _():
            q_down(l, t).wait_recv()

    def attend(l, t, near):
        def one_head(h, carry):
            q = q_ref[l, h] if near else q_all[l, t, h]
            cols = pl.ds(pl.multiple_of(h * 2 * HD, 2 * HD), HD)
            value_cols = pl.ds(pl.multiple_of(h * 2 * HD + HD, HD), HD)

            def add(state, k, v, keep):
                old, total, acc = state
                s = lax.dot_general(
                    k, q, (((1,), (1,)), ((), ())), preferred_element_type=jnp.float32
                )
                s = jnp.where(keep(s.shape), s, MASKED)
                fresh = jnp.maximum(old, jnp.max(s, 0, keepdims=True))
                p = jnp.exp2((s - fresh) * EXP_SCALE)
                fade = jnp.exp2((old - fresh) * EXP_SCALE)
                total = total * fade + jnp.sum(p, 0, keepdims=True)
                acc = acc * fade + lax.dot_general(
                    v, p.astype(jnp.bfloat16), (((0,), (0,)), ((), ())),
                    preferred_element_type=jnp.float32,
                )
                return fresh, total, acc

            state = (
                jnp.full((1, rows), EMPTY, jnp.float32),
                jnp.zeros((1, rows), jnp.float32),
                jnp.zeros((HD, rows), jnp.float32),
            )
            if near:
                def causal(shape):
                    token = lax.broadcasted_iota(jnp.int32, shape, 1) % new_count
                    return lax.broadcasted_iota(jnp.int32, shape, 0) <= token

                state = add(state, new_ref[l, :, cols], new_ref[l, :, value_cols], causal)
            for which, ref in ((0, local_ref), (1, other)):
                length = counts[l, which, t] * block_len
                state = add(
                    state, ref[l, t, :, cols], ref[l, t, :, value_cols],
                    lambda shape: lax.broadcasted_iota(jnp.int32, shape, 0) < length,
                )
            part[l, t, h] = state[2].astype(jnp.bfloat16)
            stat[l, t, h, 0:1] = state[0]
            stat[l, t, h, 1:2] = state[1]
            return carry

        lax.fori_loop(0, heads, one_head, 0)

    def p_copies(l, step, up):
        t = pairs - step if up else step
        lands, stats = (high, high_stat) if up else (low, low_stat)
        device = lax.rem(me + 2 if up else me + pool_size - 2, pool_size)
        side = int(up)
        return (
            remote(part.at[l, t], lands.at[l, step], p_send.at[l, side, step, 0],
                   p_recv.at[l, side, step, 0], device),
            remote(stat.at[l, t], stats.at[l, step], p_send.at[l, side, step, 1],
                   p_recv.at[l, side, step, 1], device),
        )

    def p_wait(l, step, up):
        for copy in p_copies(l, step, up):
            copy.wait_recv()

    def fold(l, t, step, up):
        lands, stats = (high, high_stat) if up else (low, low_stat)
        for h in range(heads):
            mine, theirs = stat[l, t, h, 0:1], stats[l, step, h, 0:1]
            top = jnp.maximum(mine, theirs)
            a, b = jnp.exp2((mine - top) * EXP_SCALE), jnp.exp2((theirs - top) * EXP_SCALE)
            part[l, t, h] = (
                part[l, t, h].astype(jnp.float32) * a + lands[l, step, h].astype(jnp.float32) * b
            ).astype(jnp.bfloat16)
            stat[l, t, h, 0:1] = top
            stat[l, t, h, 1:2] = stat[l, t, h, 1:2] * a + stats[l, step, h, 1:2] * b

    def sends(step, up):
        return line < step if up else line + step >= pairs

    def has_source(up):
        return line >= 1 if up else line <= pairs - 2

    def p_step(l, step):
        for up in (False, True):
            t = pairs - step if up else step

            @pl.when(sends(step, up))
            def _(up=up, t=t):
                if step > 1:
                    @pl.when(has_source(up))
                    def _():
                        p_wait(l, step - 1, up)
                        fold(l, t, step - 1, up)
                for copy in p_copies(l, step, up):
                    copy.start()

    def finish(l):
        for up in (False, True):
            @pl.when(has_source(up))
            def _(up=up):
                p_wait(l, pairs - 1, up)
                fold(l, 0, pairs - 1, up)
        for h in range(heads):
            done = part[l, 0, h].astype(jnp.float32) / stat[l, 0, h, 1:2]
            for g in range(GROUP):
                piece = done[:, g * new_count : (g + 1) * new_count].T
                first = (h * GROUP + g) * HD
                out_ref[l, :, first : first + HD] = piece.astype(jnp.bfloat16)

    order = [1, 3, 2]
    q_step(0, 1)
    for l in range(layers):
        kv_copy(l, 0).start()
    q_step(1, 1)
    for l in range(layers):
        for t in order:
            kv_copy(l, t).start()
    for d in range(1, WSLOTS):
        back_copy(d).start()
    kv_copy(0, 0).wait_recv()
    attend(0, 0, True)
    q_step(0, 2)
    kv_copy(1, 0).wait_recv()
    attend(1, 0, True)
    q_step(0, 3)
    q_step(1, 2)
    for n, t in enumerate(order):
        kv_copy(0, t).wait_recv()
        wait_query(0, t)
        attend(0, t, False)
        if n == 0:
            q_step(1, 3)
    p_step(0, 1)
    for n, t in enumerate(order):
        kv_copy(1, t).wait_recv()
        wait_query(1, t)
        attend(1, t, False)
        if n < 2:
            p_step(0, n + 2)
    p_step(1, 1)
    finish(0)
    for step in range(2, pairs):
        p_step(1, step)
    for d in range(WSLOTS):
        if d:
            back_copy(d).wait_recv()
        for l in range(layers):
            written_ref[l, d] = landed[d, l] if d else back_ref[d, l]
    finish(1)
    for l in range(layers):
        for t in range(pairs):
            kv_copy(l, t).wait_send()
        for step in range(1, pairs):
            pl.when(goes_down(step))(lambda: q_down(l, step).wait_send())
            pl.when(goes_up(step))(lambda: q_up(l, step).wait_send())
            for up in (False, True):
                @pl.when(sends(step, up))
                def _(up=up):
                    for copy in p_copies(l, step, up):
                        copy.wait_send()
    for d in range(1, WSLOTS):
        back_copy(d).wait_send()


def pair_attention(pool_size, block_len, counts, asked, sent, local, new_rows, back):
    layers, heads, rows, _ = asked.shape
    pairs = pool_size // 2
    new_count = new_rows.shape[1]
    vmem = pl.BlockSpec(memory_space=pltpu.VMEM)
    dma = pltpu.SemaphoreType.DMA
    sums = pltpu.VMEM((layers, pairs, heads, HD, rows), jnp.bfloat16)
    stats = pltpu.VMEM((layers, pairs, heads, 8, rows), jnp.float32)
    return pl.pallas_call(
        functools.partial(pair_kernel, pool_size, block_len),
        out_shape=(
            jax.ShapeDtypeStruct((layers, new_count, heads * GROUP * HD), jnp.bfloat16),
            jax.ShapeDtypeStruct((layers, WSLOTS) + back.shape[2:], jnp.bfloat16),
        ),
        in_specs=[pl.BlockSpec(memory_space=pltpu.SMEM), vmem,
                  pl.BlockSpec(memory_space=pl.ANY), vmem, vmem, vmem],
        out_specs=(vmem, vmem),
        scratch_shapes=[
            pltpu.VMEM((layers, pairs, heads, rows, HD), jnp.bfloat16),
            pltpu.VMEM(local.shape, jnp.bfloat16),
            sums, stats, sums, stats, sums, stats,
            pltpu.VMEM(back.shape, jnp.bfloat16),
            dma((layers, pairs)), dma((layers, pairs)),
            dma((layers, 2, pairs)), dma((layers, pairs)),
            dma((layers, 2, pairs, 2)), dma((layers, 2, pairs, 2)),
            dma((WSLOTS,)), dma((WSLOTS,)),
        ],
        compiler_params=pltpu.CompilerParams(
            collective_id=0, has_side_effects=True, vmem_limit_bytes=56 * 1024 * 1024
        ),
    )(counts, asked, sent, local, new_rows, back)


def per_device_rows(pool_size, queries, new_kv, store, fetch_list, prefix_blocks, writeback_map):
    pair_count = pool_size // 2
    me = lax.axis_index("pool")
    line, side = me // 2, me % 2
    layers, _, new_count, _ = queries.shape
    sessions = prefix_blocks.shape[0]
    slots, block_len, row_width = store.shape[1:]
    heads = row_width // (2 * HD)
    cap = MAXB // pool_size

    length = prefix_blocks[me]
    places = (length * block_len + jnp.arange(new_count, dtype=jnp.int32)).astype(jnp.float32)
    asked = []
    for layer in range(layers):
        turned = rotate(
            queries[layer, 0].reshape(new_count, heads, GROUP, HD).astype(jnp.float32),
            places[:, None, None],
        ).astype(jnp.bfloat16)
        asked.append(turned.transpose(1, 2, 0, 3).reshape(heads, GROUP * new_count, HD))

    live = jnp.arange(MAXB, dtype=jnp.int32)[None, :] < prefix_blocks[:, None]
    earlier = jnp.triu(jnp.ones((MAXB, MAXB), jnp.float32), 1)

    def used(owner):
        return (fetch_list[..., 0] == owner) & live[None]

    mine = used(me)
    rank = jnp.dot(mine.astype(jnp.float32), earlier).astype(jnp.int32)
    lanes = jnp.arange(cap, dtype=jnp.int32)
    chosen = mine[:, :, None, :] & (rank[:, :, None, :] == lanes[:, None])
    picked = jnp.sum(jnp.where(chosen, fetch_list[:, :, None, :, 1], 0), -1)
    picked = picked + (jnp.arange(layers, dtype=jnp.int32) * slots)[:, None, None]
    picked = picked.reshape(layers, pair_count, 2, cap)
    by_side = lambda a: jnp.sum(a.astype(jnp.int32), -1).reshape(layers, pair_count, 2)
    turned_lines = (line + jnp.arange(pair_count, dtype=jnp.int32)) % pair_count

    def ours(a, which):
        return jnp.take(lax.dynamic_index_in_dim(a, which, 2, False), turned_lines, axis=1)

    counts = jnp.stack(
        [ours(by_side(mine), side), ours(by_side(used(me + 1 - 2 * side)), side)], 1
    )
    flat_store = store.reshape(layers * slots, block_len, row_width)
    held = (layers, pair_count, cap * block_len, row_width)
    sent = gather_blocks(ours(picked, 1 - side).reshape(-1), flat_store).reshape(held)
    local = gather_blocks(ours(picked, side).reshape(-1), flat_store).reshape(held)
    fresh = new_kv[:, 0].reshape(layers, new_count, heads, 2, HD)
    new_keys = rotate(fresh[:, :, :, 0].astype(jnp.float32), places[:, None]).astype(jnp.bfloat16)
    new_rows = jnp.stack([new_keys, fresh[:, :, :, 1]], 3).reshape(layers, new_count, row_width)

    new_blocks = new_rows.reshape(layers, NBNEW, block_len, row_width)
    slot_of = writeback_map[:, me, :, 1]
    back = []
    for d in range(WSLOTS):
        block = jnp.zeros((layers, block_len, row_width), jnp.bfloat16)
        for b in range(NBNEW):
            block = jnp.where((slot_of[:, b] == d)[:, None, None], new_blocks[:, b], block)
        back.append(block)
    attention, written = pair_attention(
        pool_size, block_len, counts, jnp.stack(asked), sent, local, new_rows, jnp.stack(back)
    )
    return attention[:, None], written


def solution(mesh):
    pool_size = mesh.shape["pool"]
    if pool_size == 8:
        plan = functools.partial(per_device_rows, pool_size)
    else:
        plan = per_device
    in_specs = (
        P(None, ("groups", "pool"), None, "tensor"),
        P(None, ("groups", "pool"), None, "tensor"),
        P(None, ("groups", "pool"), None, "tensor"),
        P(None, "groups", None, None),
        P("groups"),
        P(None, "groups", None, None),
    )
    out_specs = (
        P(None, ("groups", "pool"), None, "tensor"),
        P(None, ("groups", "pool"), None, "tensor"),
    )
    return jax.shard_map(
        plan, mesh=mesh, in_specs=in_specs, out_specs=out_specs, check_vma=False
    )
```

```python
import functools

import jax
import jax.numpy as jnp
from jax import lax
from jax.experimental import pallas as pl
from jax.experimental.pallas import tpu as pltpu
from jax.sharding import PartitionSpec as P

HD = 128
GROUP = 8
MAXB = 64
NBNEW = 2
WSLOTS = 4


def rotate(source, places):
    half_width = source.shape[-1] // 2
    frequencies = 500000.0 ** (
        -(jnp.arange(half_width, dtype=jnp.float32) * 2.0 / source.shape[-1])
    )
    angles = places[..., None] * frequencies
    cosine = jnp.cos(angles)
    sine_part = jnp.sin(angles)
    first_half = source[..., :half_width]
    second = source[..., half_width:]
    return jnp.concatenate(
        [first_half * cosine - second * sine_part, second * cosine + first_half * sine_part], -1
    )


def per_device(queries, new_kv, store, fetch_list, prefix_blocks, writeback_map):
    pool_size = lax.axis_size("pool")
    my_index = lax.axis_index("pool")
    layer_count = queries.shape[0]
    new_count = queries.shape[2]
    block_len = store.shape[2]
    row_width = store.shape[3]
    kv_local = row_width // (2 * HD)
    per_owner = MAXB // pool_size
    score_scale = HD ** (-0.5)
    length = prefix_blocks[my_index]
    places = (length * block_len + jnp.arange(new_count, dtype=jnp.int32)).astype(jnp.float32)
    block_order = jnp.arange(MAXB, dtype=jnp.int32)
    earlier = block_order[None, :] < block_order[:, None]
    live_entries = block_order[None, :] < prefix_blocks[:, None]
    lane_ids = jnp.arange(per_owner, dtype=jnp.int32)
    sources = jnp.arange(pool_size, dtype=jnp.int32)
    slot_range = jnp.arange(WSLOTS, dtype=jnp.int32)
    token_ids = jnp.arange(new_count, dtype=jnp.int32)
    causal_rows = jnp.repeat(token_ids[None, :] <= token_ids[:, None], GROUP, axis=0)
    attention_all = []
    written_all = []
    for layer_index in range(layer_count):
        owners = fetch_list[layer_index, :, :, 0]
        slot_ids = fetch_list[layer_index, :, :, 1]
        owner_rank = jnp.sum((owners[:, :, None] == owners[:, None, :]) & earlier[None], -1)
        chosen = ((owners == my_index) & live_entries)[:, None, :] & (
            owner_rank[:, None, :] == lane_ids[None, :, None]
        )
        picked = jnp.sum(jnp.where(chosen, slot_ids[:, None, :], 0), -1).reshape(-1)
        present = jnp.any(chosen, -1).reshape(-1)
        picked_rows = jnp.take(store[layer_index], picked, axis=0)
        outgoing = jnp.where(present[:, None, None], picked_rows, jnp.zeros_like(picked_rows))
        arrival = (
            (owners[my_index][:, None, None] == sources[None, :, None])
            & (owner_rank[my_index][:, None, None] == lane_ids[None, None, :])
            & live_entries[my_index][:, None, None]
        )
        outgoing, prefix_ok = (outgoing, jnp.any(arrival, 0).reshape(-1))
        prefix = lax.all_to_all(outgoing, "pool", split_axis=0, concat_axis=0, tiled=True)
        rotated_query = rotate(
            queries[layer_index, 0].reshape(new_count, kv_local, GROUP, HD).astype(jnp.float32),
            places[:, None, None],
        ).astype(jnp.bfloat16)
        fresh_rows = new_kv[layer_index, 0].reshape(new_count, kv_local, 2, HD)
        new_keys = rotate(fresh_rows[:, :, 0].astype(jnp.float32), places[:, None]).astype(
            jnp.bfloat16
        )
        values = fresh_rows[:, :, 1]
        key_count = prefix.shape[0] * prefix.shape[1]
        flat_prefix = prefix.reshape(key_count, kv_local, 2, HD)
        kept_keys = jnp.repeat(prefix_ok, prefix.shape[1])
        results = []
        for head_index in range(kv_local):
            query_rows = rotated_query[:, head_index].reshape(new_count * GROUP, HD)
            far_scores = (
                jnp.einsum(
                    "rd,nd->rn",
                    query_rows,
                    flat_prefix[:, head_index, 0],
                    preferred_element_type=jnp.float32,
                )
                * score_scale
            )
            near_scores = (
                jnp.einsum(
                    "rd,nd->rn",
                    query_rows,
                    new_keys[:, head_index],
                    preferred_element_type=jnp.float32,
                )
                * score_scale
            )
            far_scores = jnp.where(kept_keys[None, :], far_scores, -jnp.inf)
            near_scores = jnp.where(causal_rows, near_scores, -jnp.inf)
            row_top = jnp.maximum(jnp.max(far_scores, -1), jnp.max(near_scores, -1))
            far_weights = jnp.exp(far_scores - row_top[:, None])
            near_weights = jnp.exp(near_scores - row_top[:, None])
            row_total = jnp.sum(far_weights, -1) + jnp.sum(near_weights, -1)
            mixture = jnp.einsum(
                "rn,nd->rd",
                far_weights.astype(jnp.bfloat16),
                flat_prefix[:, head_index, 1],
                preferred_element_type=jnp.float32,
            )
            mixture = mixture + jnp.einsum(
                "rn,nd->rd",
                near_weights.astype(jnp.bfloat16),
                values[:, head_index],
                preferred_element_type=jnp.float32,
            )
            results.append((mixture / row_total[:, None]).reshape(new_count, GROUP, HD))
        attention = (
            jnp.stack(results, 1).reshape(new_count, kv_local * GROUP * HD).astype(jnp.bfloat16)
        )
        attend_blocks = jnp.stack([new_keys, values], 2).reshape(NBNEW, block_len * row_width)
        attention, blocks = (attention, attend_blocks)
        attention_all.append(attention)
        targets = writeback_map[layer_index, :, :, 0]
        target_slots = writeback_map[layer_index, :, :, 1]
        flat_targets = targets.reshape(-1)
        flat_slots = target_slots.reshape(-1)
        selector = (
            (flat_targets == my_index)[None, :] & (flat_slots[None, :] == slot_range[:, None])
        ).astype(jnp.bfloat16)
        stored = jnp.dot(
            selector,
            lax.all_gather(blocks, "pool", axis=0, tiled=True),
            preferred_element_type=jnp.float32,
        )
        written_all.append(stored.astype(jnp.bfloat16).reshape(WSLOTS, block_len, row_width))
    return (jnp.stack(attention_all)[:, None], jnp.stack(written_all))

EMPTY = -1e30
EXP_SCALE = HD ** (-0.5) * 1.4426950408889634
MASKED = -2e30


def gather_kernel(picks, store_ref, out_ref, sems):
    count = out_ref.shape[0]

    def copy(i):
        return pltpu.make_async_copy(store_ref.at[picks[i]], out_ref.at[i], sems.at[i])

    lax.fori_loop(0, count, lambda i, x: (copy(i).start(), x)[1], 0)
    lax.fori_loop(0, count, lambda i, x: (copy(i).wait(), x)[1], 0)


def gather_blocks(picks, flat_store):
    return pl.pallas_call(
        gather_kernel,
        out_shape=jax.ShapeDtypeStruct(picks.shape + flat_store.shape[1:], flat_store.dtype),
        grid_spec=pltpu.PrefetchScalarGridSpec(
            num_scalar_prefetch=1,
            grid=(),
            in_specs=[pl.BlockSpec(memory_space=pl.ANY)],
            out_specs=pl.BlockSpec(memory_space=pltpu.VMEM),
            scratch_shapes=[pltpu.SemaphoreType.DMA(picks.shape)],
        ),
        compiler_params=pltpu.CompilerParams(vmem_limit_bytes=16 * 1024 * 1024),
    )(picks, flat_store)


def shift_of(d, pool_size):
    return d % 2 + d // 2 * (2 * pool_size // WSLOTS)


def pair_kernel(
    pool_size, block_len, counts, q_ref, sent_ref, local_ref, new_ref, back_ref,
    out_ref, written_ref,
    q_all, other, part, stat, low, low_stat, high, high_stat, landed,
    kv_send, kv_recv, q_send, q_recv, p_send, p_recv, w_send, w_recv,
):
    pairs = pool_size // 2
    layers, heads, rows, _ = q_ref.shape
    new_count = new_ref.shape[1]
    kept = local_ref.shape[2]
    me = lax.axis_index("pool")
    line = me // 2
    partner = me + 1 - 2 * (me % 2)

    def remote(src, dst, send, recv, device):
        return pltpu.make_async_remote_copy(
            src_ref=src, dst_ref=dst, send_sem=send, recv_sem=recv,
            device_id={"pool": device}, device_id_type=pl.DeviceIdType.MESH,
        )

    barrier = pltpu.get_barrier_semaphore()
    for k in range(1, pool_size):
        pl.semaphore_signal(
            barrier, inc=1, device_id={"pool": lax.rem(me + k, pool_size)},
            device_id_type=pl.DeviceIdType.MESH,
        )
    pl.semaphore_wait(barrier, pool_size - 1)

    def kv_copy(l, t):
        return remote(
            sent_ref.at[l, t], other.at[l, t], kv_send.at[l, t], kv_recv.at[l, t], partner
        )

    def q_down(l, step):
        src = q_ref.at[l] if step == 1 else q_all.at[l, step - 1]
        return remote(
            src, q_all.at[l, step], q_send.at[l, 0, step], q_recv.at[l, step],
            lax.rem(me + pool_size - 2, pool_size),
        )

    def q_up(l, step):
        src = q_ref.at[l] if step == 1 else q_all.at[l, pairs - step + 1]
        return remote(
            src, q_all.at[l, pairs - step], q_send.at[l, 1, step], q_recv.at[l, pairs - step],
            lax.rem(me + 2, pool_size),
        )

    def goes_down(step):
        return (line >= 1) & (line + step <= pairs)

    def goes_up(step):
        return (line <= pairs - 2) & (line - step + 1 >= 0)

    def back_copy(d):
        device = lax.rem(me + shift_of(d, pool_size), pool_size)
        return remote(back_ref.at[d], landed.at[d], w_send.at[d], w_recv.at[d], device)

    def q_step(l, step):
        @pl.when(goes_down(step))
        def _():
            if step > 1:
                q_down(l, step - 1).wait_recv()
            q_down(l, step).start()

        @pl.when(goes_up(step))
        def _():
            if step > 1:
                q_up(l, step - 1).wait_recv()
            q_up(l, step).start()

    def wait_query(l, t):
        from_above = line + t <= pairs - 1
        passed = jnp.where(from_above, goes_down(t + 1), goes_up(pairs - t + 1))

        @pl.when(jnp.logical_not(passed))
        def _():
            q_down(l, t).wait_recv()

    def attend(l, t, near):
        def one_head(h, carry):
            q = q_ref[l, h] if near else q_all[l, t, h]
            cols = pl.ds(pl.multiple_of(h * 2 * HD, 2 * HD), HD)
            value_cols = pl.ds(pl.multiple_of(h * 2 * HD + HD, HD), HD)

            def add(state, k, v, keep):
                old, total, acc = state
                s = lax.dot_general(
                    k, q, (((1,), (1,)), ((), ())), preferred_element_type=jnp.float32
                )
                s = jnp.where(keep(s.shape), s, MASKED)
                fresh = jnp.maximum(old, jnp.max(s, 0, keepdims=True))
                p = jnp.exp2((s - fresh) * EXP_SCALE)
                fade = jnp.exp2((old - fresh) * EXP_SCALE)
                total = total * fade + jnp.sum(p, 0, keepdims=True)
                acc = acc * fade + lax.dot_general(
                    v, p.astype(jnp.bfloat16), (((0,), (0,)), ((), ())),
                    preferred_element_type=jnp.float32,
                )
                return fresh, total, acc

            state = (
                jnp.full((1, rows), EMPTY, jnp.float32),
                jnp.zeros((1, rows), jnp.float32),
                jnp.zeros((HD, rows), jnp.float32),
            )
            if near:
                def causal(shape):
                    token = lax.broadcasted_iota(jnp.int32, shape, 1) % new_count
                    return lax.broadcasted_iota(jnp.int32, shape, 0) <= token

                state = add(state, new_ref[l, :, cols], new_ref[l, :, value_cols], causal)
            for which, ref in ((0, local_ref), (1, other)):
                length = counts[l, which, t] * block_len
                state = add(
                    state, ref[l, t, :, cols], ref[l, t, :, value_cols],
                    lambda shape: lax.broadcasted_iota(jnp.int32, shape, 0) < length,
                )
            part[l, t, h] = state[2].astype(jnp.bfloat16)
            stat[l, t, h, 0:1] = state[0]
            stat[l, t, h, 1:2] = state[1]
            return carry

        lax.fori_loop(0, heads, one_head, 0)

    def p_copies(l, step, up):
        t = pairs - step if up else step
        lands, stats = (high, high_stat) if up else (low, low_stat)
        device = lax.rem(me + 2 if up else me + pool_size - 2, pool_size)
        side = int(up)
        return (
            remote(part.at[l, t], lands.at[l, step], p_send.at[l, side, step, 0],
                   p_recv.at[l, side, step, 0], device),
            remote(stat.at[l, t], stats.at[l, step], p_send.at[l, side, step, 1],
                   p_recv.at[l, side, step, 1], device),
        )

    def p_wait(l, step, up):
        for copy in p_copies(l, step, up):
            copy.wait_recv()

    def fold(l, t, step, up):
        lands, stats = (high, high_stat) if up else (low, low_stat)
        for h in range(heads):
            mine, theirs = stat[l, t, h, 0:1], stats[l, step, h, 0:1]
            top = jnp.maximum(mine, theirs)
            a, b = jnp.exp2((mine - top) * EXP_SCALE), jnp.exp2((theirs - top) * EXP_SCALE)
            part[l, t, h] = (
                part[l, t, h].astype(jnp.float32) * a + lands[l, step, h].astype(jnp.float32) * b
            ).astype(jnp.bfloat16)
            stat[l, t, h, 0:1] = top
            stat[l, t, h, 1:2] = stat[l, t, h, 1:2] * a + stats[l, step, h, 1:2] * b

    def sends(step, up):
        return line < step if up else line + step >= pairs

    def has_source(up):
        return line >= 1 if up else line <= pairs - 2

    def p_step(l, step):
        for up in (False, True):
            t = pairs - step if up else step

            @pl.when(sends(step, up))
            def _(up=up, t=t):
                if step > 1:
                    @pl.when(has_source(up))
                    def _():
                        p_wait(l, step - 1, up)
                        fold(l, t, step - 1, up)
                for copy in p_copies(l, step, up):
                    copy.start()

    def finish(l):
        for up in (False, True):
            @pl.when(has_source(up))
            def _(up=up):
                p_wait(l, pairs - 1, up)
                fold(l, 0, pairs - 1, up)
        for h in range(heads):
            done = part[l, 0, h].astype(jnp.float32) / stat[l, 0, h, 1:2]
            for g in range(GROUP):
                piece = done[:, g * new_count : (g + 1) * new_count].T
                first = (h * GROUP + g) * HD
                out_ref[l, :, first : first + HD] = piece.astype(jnp.bfloat16)

    order = [1, 3, 2]
    q_step(0, 1)
    for l in range(layers):
        kv_copy(l, 0).start()
    q_step(1, 1)
    for l in range(layers):
        for t in order:
            kv_copy(l, t).start()
    for d in range(1, WSLOTS):
        back_copy(d).start()
    kv_copy(0, 0).wait_recv()
    attend(0, 0, True)
    q_step(0, 2)
    kv_copy(1, 0).wait_recv()
    attend(1, 0, True)
    q_step(0, 3)
    q_step(1, 2)
    for n, t in enumerate(order):
        kv_copy(0, t).wait_recv()
        wait_query(0, t)
        attend(0, t, False)
        if n == 0:
            q_step(1, 3)
        if n == 1:
            p_step(0, 1)
    for n, t in enumerate(order):
        kv_copy(1, t).wait_recv()
        wait_query(1, t)
        attend(1, t, False)
        if n < 2:
            p_step(0, n + 2)
        if n == 1:
            p_step(1, 1)
    p_step(1, 2)
    finish(0)
    p_step(1, 3)
    for d in range(WSLOTS):
        if d:
            back_copy(d).wait_recv()
        for l in range(layers):
            written_ref[l, d] = landed[d, l] if d else back_ref[d, l]
    finish(1)
    for l in range(layers):
        for t in range(pairs):
            kv_copy(l, t).wait_send()
        for step in range(1, pairs):
            pl.when(goes_down(step))(lambda: q_down(l, step).wait_send())
            pl.when(goes_up(step))(lambda: q_up(l, step).wait_send())
            for up in (False, True):
                @pl.when(sends(step, up))
                def _(up=up):
                    for copy in p_copies(l, step, up):
                        copy.wait_send()
    for d in range(1, WSLOTS):
        back_copy(d).wait_send()


def pair_attention(pool_size, block_len, counts, asked, sent, local, new_rows, back):
    layers, heads, rows, _ = asked.shape
    pairs = pool_size // 2
    new_count = new_rows.shape[1]
    vmem = pl.BlockSpec(memory_space=pltpu.VMEM)
    dma = pltpu.SemaphoreType.DMA
    sums = pltpu.VMEM((layers, pairs, heads, HD, rows), jnp.bfloat16)
    stats = pltpu.VMEM((layers, pairs, heads, 8, rows), jnp.float32)
    return pl.pallas_call(
        functools.partial(pair_kernel, pool_size, block_len),
        out_shape=(
            jax.ShapeDtypeStruct((layers, new_count, heads * GROUP * HD), jnp.bfloat16),
            jax.ShapeDtypeStruct((layers, WSLOTS) + back.shape[2:], jnp.bfloat16),
        ),
        in_specs=[pl.BlockSpec(memory_space=pltpu.SMEM), vmem,
                  pl.BlockSpec(memory_space=pl.ANY), vmem, vmem, vmem],
        out_specs=(vmem, vmem),
        scratch_shapes=[
            pltpu.VMEM((layers, pairs, heads, rows, HD), jnp.bfloat16),
            pltpu.VMEM(local.shape, jnp.bfloat16),
            sums, stats, sums, stats, sums, stats,
            pltpu.VMEM(back.shape, jnp.bfloat16),
            dma((layers, pairs)), dma((layers, pairs)),
            dma((layers, 2, pairs)), dma((layers, pairs)),
            dma((layers, 2, pairs, 2)), dma((layers, 2, pairs, 2)),
            dma((WSLOTS,)), dma((WSLOTS,)),
        ],
        compiler_params=pltpu.CompilerParams(
            collective_id=0, has_side_effects=True, vmem_limit_bytes=56 * 1024 * 1024
        ),
    )(counts, asked, sent, local, new_rows, back)


def per_device_rows(pool_size, queries, new_kv, store, fetch_list, prefix_blocks, writeback_map):
    pair_count = pool_size // 2
    me = lax.axis_index("pool")
    line, side = me // 2, me % 2
    layers, _, new_count, _ = queries.shape
    sessions = prefix_blocks.shape[0]
    slots, block_len, row_width = store.shape[1:]
    heads = row_width // (2 * HD)
    cap = MAXB // pool_size

    length = prefix_blocks[me]
    places = (length * block_len + jnp.arange(new_count, dtype=jnp.int32)).astype(jnp.float32)
    asked = []
    for layer in range(layers):
        turned = rotate(
            queries[layer, 0].reshape(new_count, heads, GROUP, HD).astype(jnp.float32),
            places[:, None, None],
        ).astype(jnp.bfloat16)
        asked.append(turned.transpose(1, 2, 0, 3).reshape(heads, GROUP * new_count, HD))

    live = jnp.arange(MAXB, dtype=jnp.int32)[None, :] < prefix_blocks[:, None]
    earlier = jnp.triu(jnp.ones((MAXB, MAXB), jnp.float32), 1)

    def used(owner):
        return (fetch_list[..., 0] == owner) & live[None]

    mine = used(me)
    rank = jnp.dot(mine.astype(jnp.float32), earlier).astype(jnp.int32)
    lanes = jnp.arange(cap, dtype=jnp.int32)
    chosen = mine[:, :, None, :] & (rank[:, :, None, :] == lanes[:, None])
    picked = jnp.sum(jnp.where(chosen, fetch_list[:, :, None, :, 1], 0), -1)
    picked = picked + (jnp.arange(layers, dtype=jnp.int32) * slots)[:, None, None]
    picked = picked.reshape(layers, pair_count, 2, cap)
    by_side = lambda a: jnp.sum(a.astype(jnp.int32), -1).reshape(layers, pair_count, 2)
    turned_lines = (line + jnp.arange(pair_count, dtype=jnp.int32)) % pair_count

    def ours(a, which):
        return jnp.take(lax.dynamic_index_in_dim(a, which, 2, False), turned_lines, axis=1)

    counts = jnp.stack(
        [ours(by_side(mine), side), ours(by_side(used(me + 1 - 2 * side)), side)], 1
    )
    flat_store = store.reshape(layers * slots, block_len, row_width)
    held = (layers, pair_count, cap * block_len, row_width)
    sent = gather_blocks(ours(picked, 1 - side).reshape(-1), flat_store).reshape(held)
    local = gather_blocks(ours(picked, side).reshape(-1), flat_store).reshape(held)
    fresh = new_kv[:, 0].reshape(layers, new_count, heads, 2, HD)
    new_keys = rotate(fresh[:, :, :, 0].astype(jnp.float32), places[:, None]).astype(jnp.bfloat16)
    new_rows = jnp.stack([new_keys, fresh[:, :, :, 1]], 3).reshape(layers, new_count, row_width)

    new_blocks = new_rows.reshape(layers, NBNEW, block_len, row_width)
    slot_of = writeback_map[:, me, :, 1]
    back = []
    for d in range(WSLOTS):
        block = jnp.zeros((layers, block_len, row_width), jnp.bfloat16)
        for b in range(NBNEW):
            block = jnp.where((slot_of[:, b] == d)[:, None, None], new_blocks[:, b], block)
        back.append(block)
    attention, written = pair_attention(
        pool_size, block_len, counts, jnp.stack(asked), sent, local, new_rows, jnp.stack(back)
    )
    return attention[:, None], written


def solution(mesh):
    pool_size = mesh.shape["pool"]
    if pool_size == 8:
        plan = functools.partial(per_device_rows, pool_size)
    else:
        plan = per_device
    in_specs = (
        P(None, ("groups", "pool"), None, "tensor"),
        P(None, ("groups", "pool"), None, "tensor"),
        P(None, ("groups", "pool"), None, "tensor"),
        P(None, "groups", None, None),
        P("groups"),
        P(None, "groups", None, None),
    )
    out_specs = (
        P(None, ("groups", "pool"), None, "tensor"),
        P(None, ("groups", "pool"), None, "tensor"),
    )
    return jax.shard_map(
        plan, mesh=mesh, in_specs=in_specs, out_specs=out_specs, check_vma=False
    )
```
